32 devices in a mesh: groups: 2 (over y), gx: 4 (over z), gy: 4 (over x, core).
Axes of the slice: x: 2, y: 2, z: 4, core: 2. Of those that a mesh axis runs over, the one named last changes fastest.
Arguments:
- local_grad: float32 [49, 32, 16, 32], P(None, ('groups', 'gx'), 'gy'), parts along dimension 1, may hold values from -6 to 6
- translation: bfloat16 [7, 7, 7, 49, 49], replicated, may hold values from -0.0625 to 0.0625
- basis: bfloat16 [49, 131072], P(None, ('groups', 'gx', 'gy')), parts along dimension 1, may hold values from -0.875 to 0.875
- basis_grad: bfloat16 [3, 49, 131072], P(None, None, ('groups', 'gx', 'gy')), parts along dimension 2, may hold values from -0.875 to 0.875
- charges: float32 [131072], P(('groups', 'gx', 'gy')), parts along dimension 0, may hold values from -5 to 5
- atom_leaf: int32 [131072], P(('groups', 'gx', 'gy')), parts along dimension 0, may hold values from 0 to 8191, as said below
Outputs:
- leaf_mgrad: float32 [49, 32, 16, 32], P(None, ('groups', 'gx'), 'gy'), parts along dimension 1
- charge_grad: float32 [131072], P(('groups', 'gx', 'gy')), parts along dimension 0
- forces: float32 [3, 131072], P(None, ('groups', 'gx', 'gy')), parts along dimension 1
The draws below stay inside these ranges and needn't reach their ends.
There are 2 independent parts, one for each index of `groups`. The reference program is written for one: setup_inputs(seed, part) draws one part's arguments, and reference() takes and returns one part's arrays. A program takes and returns all parts, laid end to end along the dimension named above; an argument that names none is the same for every part. Nothing has to cross between parts.
Inputs may be any that keep to these rules, and one draw needn't show every extreme that they name: atom_leaf[i] = (x * 16 + y) * 32 + z for the leaf box (x, y, z) of atom i; that box lies in the block of leaf boxes of the device that holds the atom or in a box next to that block.
All inputs are finite; a program needn't handle non-finite values.
Results may differ from the reference program's by a relative error of at most 0.0041.
Values may be sent and summed in bfloat16 or wider, within the bound.
A program may use at most 128 MiB of HBM per device.

```python
import jax
import jax.numpy as jnp
from jax import lax

P_SIZE = 49
CX = 4
CY = 4
A_DEV = 4096
NX = 16
NY = 16
NZ = 32
ATOMS = 65536


def draw_atom_leaf(key, part):
    key = jax.random.fold_in(key, 11)
    slot_index = jnp.arange(ATOMS, dtype=jnp.int32)
    device = slot_index // A_DEV
    columns = NY // CY
    block_x = device // columns
    block_y = device % columns
    key_x, key_y, key_z = jax.random.split(key, 3)
    off_x = jax.random.randint(key_x, (ATOMS,), -1, CX + 1, dtype=jnp.int32)
    off_y = jax.random.randint(key_y, (ATOMS,), -1, CY + 1, dtype=jnp.int32)
    leaf_z = jax.random.randint(key_z, (ATOMS,), 0, NZ, dtype=jnp.int32)
    leaf_x = jnp.clip(block_x * CX + off_x, 0, NX - 1)
    leaf_y = jnp.clip(block_y * CY + off_y, 0, NY - 1)
    leaf_id = (leaf_x * NY + leaf_y) * NZ + leaf_z
    leaf_id = jnp.where(slot_index == 0, 0, leaf_id)
    leaf_id = jnp.where(slot_index == ATOMS - 1, NX * NY * NZ - 1, leaf_id)
    return leaf_id.astype(jnp.int32)


def shard_levels(rng, shape, cuts, low, largest):
    def one(position, parts):
        heights = jax.random.uniform(jax.random.fold_in(jax.random.fold_in(rng, 6), position), (parts,), jnp.float32, low / len(cuts), largest / len(cuts))
        return jnp.repeat(jnp.exp(heights), shape[position] // parts).reshape((-1,) + (1,) * (len(shape) - position - 1))

    factor_of = one(*cuts[0])
    for cut in cuts[1:]:
        factor_of = factor_of * one(*cut)
    return factor_of


def scatter_about(own_key, shape, spread, reach, cuts=(), kind=jnp.bfloat16):
    array = spread * jax.random.normal(own_key, shape, jnp.float32)
    if cuts:
        array = array * shard_levels(own_key, shape, cuts, -0.22, 0.18)
    return jnp.clip(array, -reach, reach).astype(kind)


def setup_inputs(seed: int = 0, part: int = 0) -> dict:
    streams_of = jax.random.split(jax.random.key(seed), 7)
    own_keys = jax.random.split(jax.random.fold_in(streams_of[6], part), 7)
    local_grad = scatter_about(own_keys[0], (P_SIZE, NX, NY, NZ), 1.0, 6.0, ((1, 4), (2, 4)), jnp.float32)
    translation = scatter_about(streams_of[1], (7, 7, 7, P_SIZE, P_SIZE), (P_SIZE * 189) ** -0.5, 0.0625)
    basis = scatter_about(own_keys[2], (P_SIZE, ATOMS), P_SIZE ** -0.5, 0.875, ((1, 16),))
    basis_grad = scatter_about(own_keys[3], (3, P_SIZE, ATOMS), P_SIZE ** -0.5, 0.875, ((2, 16),))
    charges = scatter_about(own_keys[4], (ATOMS,), 1.0, 5.0, ((0, 16),), jnp.float32)
    atom_leaf = draw_atom_leaf(jax.random.fold_in(jax.random.fold_in(streams_of[6], part), 71), part)
    return dict(local_grad=local_grad, translation=translation, basis=basis, basis_grad=basis_grad, charges=charges, atom_leaf=atom_leaf)


def class_kernel(translation):
    extent = translation.shape[0]
    offset = jnp.abs(jnp.arange(extent) - 3)
    far_mask = (offset[:, None, None] >= 2) | (offset[None, :, None] >= 2) | (offset[None, None, :] >= 2)
    masked = translation * far_mask[:, :, :, None, None].astype(translation.dtype)
    pieces = []
    for parity_x in range(2):
        for parity_y in range(2):
            for parity_z in range(2):
                sliced = masked[parity_x:parity_x + 6, parity_y:parity_y + 6, parity_z:parity_z + 6]
                pieces.append(sliced[::-1, ::-1, ::-1])
    stacked = jnp.stack(pieces, axis=4)
    coeffs = translation.shape[3]
    return stacked.reshape(6, 6, 6, coeffs, 8 * coeffs)


def far_adjoint(padded, kernel):
    coeffs = padded.shape[0]
    source = padded[None, :, 1:, 1:, 1:]
    result = lax.conv_general_dilated(source, kernel, (2, 2, 2), "VALID", dimension_numbers=("NCDHW", "DHWIO", "NCDHW"), preferred_element_type=jnp.float32)
    half_x, half_y, half_z = result.shape[2], result.shape[3], result.shape[4]
    result = result.reshape(2, 2, 2, coeffs, half_x, half_y, half_z)
    result = jnp.transpose(result, (3, 4, 0, 5, 1, 6, 2))
    return result.reshape(coeffs, 2 * half_x, 2 * half_y, 2 * half_z)


def reference(local_grad, translation, basis, basis_grad, charges, atom_leaf):
    rounded = local_grad.astype(jnp.bfloat16)
    padded = jnp.pad(rounded, ((0, 0), (3, 3), (3, 3), (3, 3)))
    leaf_mgrad = far_adjoint(padded, class_kernel(translation))
    box_grad = leaf_mgrad.astype(jnp.bfloat16).reshape(P_SIZE, -1)
    gathered = jnp.take(box_grad, atom_leaf, axis=1).astype(jnp.float32)
    charge_grad = jnp.sum(basis.astype(jnp.float32) * gathered, axis=0)
    forces = -charges[None, :] * jnp.sum(basis_grad.astype(jnp.float32) * gathered[None], axis=1)
    return leaf_mgrad, charge_grad, forces
```

```python
import jax
import jax.numpy as jnp
from jax import lax
from jax.experimental import pallas as pl
from jax.experimental.pallas import tpu as pltpu
from jax.sharding import PartitionSpec as P

MESH = pl.DeviceIdType.MESH
LANES = 128
HALF = 64
DIRS = ((-1, 0), (1, 0), (0, -1), (0, 1), (-1, -1), (-1, 1), (1, -1), (1, 1))


def source_span(step, width, depth):
    if step == 0:
        return depth, width
    return (depth, depth) if step < 0 else (width, depth)


def target_span(step, width, depth):
    if step == 0:
        return depth, width
    return (width + depth, depth) if step < 0 else (0, depth)


def kernel(
    count_x,
    count_y,
    grad_hbm,
    trans_hbm,
    basis_hbm,
    bgrad_hbm,
    charges_ref,
    leaf_ref,
    mgrad_hbm,
    charge_ref,
    forces_ref,
    grad,
    wide,
    trans,
    basis,
    bgrad,
    packed,
    windows,
    weights,
    mgrad_wide,
    mgrad,
    boxes,
    picked,
    place,
    load_sem,
    trans_sem,
    send_sem,
    recv_sem,
    send2_sem,
    recv2_sem,
    out_sem,
):
    width_x, width_y, depth_z, coeffs = grad.shape
    pairs = depth_z // 2
    extent = trans.shape[0]
    atoms = leaf_ref.shape[1]
    gx, gy = lax.axis_index("gx"), lax.axis_index("gy")

    grad_copy = pltpu.make_async_copy(grad_hbm, grad, load_sem.at[0])
    grad_copy.start()
    for dx in range(extent):
        pltpu.make_async_copy(trans_hbm.at[dx], trans.at[dx], trans_sem.at[dx]).start()
    basis_copy = pltpu.make_async_copy(basis_hbm, basis, load_sem.at[1])
    bgrad_copy = pltpu.make_async_copy(bgrad_hbm, bgrad, load_sem.at[2])
    basis_copy.start()
    bgrad_copy.start()

    def exists(sx, sy):
        ok = None
        for here, step, count in ((gx, sx, count_x), (gy, sy, count_y)):
            if step:
                test = (here + step >= 0) & (here + step < count)
                ok = test if ok is None else ok & test
        return ok

    barrier = pltpu.get_barrier_semaphore()
    for sx, sy in DIRS:
        @pl.when(exists(sx, sy))
        def _():
            pl.semaphore_signal(
                barrier, inc=1, device_id={"gx": gx + sx, "gy": gy + sy}, device_id_type=MESH
            )

    def spans(which, sx, sy, depth):
        (x0, nx), (y0, ny) = which(sx, width_x, depth), which(sy, width_y, depth)
        return pl.ds(x0, nx), pl.ds(y0, ny)

    def exchange1(k):
        sx, sy = DIRS[k]
        src = spans(source_span, sx, sy, 2)
        dst = spans(target_span, sx, sy, 2)
        return pltpu.make_async_remote_copy(
            src_ref=packed.at[src[0], src[1]],
            dst_ref=packed.at[dst[0], dst[1]],
            send_sem=send_sem.at[k],
            recv_sem=recv_sem.at[k],
            device_id={"gx": gx + sx, "gy": gy + sy},
            device_id_type=MESH,
        )

    def exchange2(k):
        sx, sy = DIRS[k]
        src = spans(source_span, sx, sy, 1)
        dst = spans(target_span, sx, sy, 1)
        return pltpu.make_async_remote_copy(
            src_ref=boxes.at[src[0], src[1]],
            dst_ref=boxes.at[dst[0], dst[1]],
            send_sem=send2_sem.at[k],
            recv_sem=recv2_sem.at[k],
            device_id={"gx": gx + sx, "gy": gy + sy},
            device_id_type=MESH,
        )

    wide[...] = jnp.zeros_like(wide)
    grad_copy.wait()
    wide[:, :, :, :coeffs] = grad[...]
    for x in range(width_x):
        for y in range(width_y):
            even = wide[x, y, pl.ds(0, pairs, stride=2), :]
            odd = wide[x, y, pl.ds(1, pairs, stride=2), :]
            both = odd + pltpu.roll(even, HALF, 1)
            packed[2 + x, 2 + y] = both.astype(jnp.bfloat16)

    def span_of(here, count):
        return jnp.minimum(here + 1, count - 1) - jnp.maximum(here - 1, 0) + 1

    pl.semaphore_wait(barrier, span_of(gx, count_x) * span_of(gy, count_y) - 1)

    for k, (sx, sy) in enumerate(DIRS):
        @pl.when(exists(sx, sy))
        def _():
            exchange1(k).start()

        @pl.when(jnp.logical_not(exists(sx, sy)))
        def _():
            x, y = spans(target_span, -sx, -sy, 2)
            packed[x, y] = jnp.zeros((x.size, y.size, pairs, LANES), jnp.bfloat16)
            x, y = spans(target_span, -sx, -sy, 1)
            boxes[x, y] = jnp.zeros((x.size, y.size, pairs, LANES), jnp.bfloat16)

    leaf = leaf_ref[...]
    rows_y = width_y * count_y
    plane = rows_y * depth_z
    lx = leaf // plane - gx * width_x
    ly = leaf // depth_z % rows_y - gy * width_y
    z = leaf % depth_z
    in_x = (lx >= 0) & (lx < width_x)
    in_y = (ly >= 0) & (ly < width_y)
    own_cols = width_x * width_y
    face_x = jnp.where(lx < 0, 0, width_y) + ly
    face_y = 2 * width_y + jnp.where(ly < 0, 0, width_x) + lx
    corner = 2 * (width_x + width_y) + jnp.where(lx < 0, 0, 2) + jnp.where(ly < 0, 0, 1)
    column = jnp.where(
        in_x & in_y,
        lx * width_y + ly,
        own_cols + jnp.where(in_y, face_x, jnp.where(in_x, face_y, corner)),
    )
    place[0:1, :] = column * pairs + z // 2
    place[1:2, :] = z % 2

    def prepare(dx, carry):
        pltpu.make_async_copy(trans_hbm.at[dx], trans.at[dx], trans_sem.at[dx]).wait()
        for dy in range(extent):
            blocks = []
            for dz in range(extent):
                one = trans[dx, dy, dz]
                blocks.append(jnp.pad(one, ((0, HALF - coeffs), (0, HALF - coeffs))))
            for m in range(extent - 1):
                weights[dx, dy, m * HALF : (m + 1) * HALF, :] = jnp.concatenate(
                    [blocks[m], blocks[m + 1]], axis=1
                )
        return carry

    lax.fori_loop(0, extent, prepare, 0)
    low_lanes = lax.broadcasted_iota(jnp.int32, (HALF, LANES), 1) < HALF
    for dx in range(2, extent - 2):
        for dy in range(2, extent - 2):
            first, last = pl.ds(HALF, HALF), pl.ds(4 * HALF, HALF)
            head = weights[dx, dy, first, :].astype(jnp.float32)
            weights[dx, dy, first, :] = jnp.where(low_lanes, head, 0.0).astype(jnp.bfloat16)
            weights[dx, dy, pl.ds(2 * HALF, 2 * HALF), :] = jnp.zeros(
                (2 * HALF, LANES), jnp.bfloat16
            )
            tail = weights[dx, dy, last, :].astype(jnp.float32)
            weights[dx, dy, last, :] = jnp.where(low_lanes, 0.0, tail).astype(jnp.bfloat16)

    for k, (sx, sy) in enumerate(DIRS):
        @pl.when(exists(-sx, -sy))
        def _():
            exchange1(k).wait_recv()

    row = lax.broadcasted_iota(jnp.int32, (pairs, LANES), 0)

    def window(x, carry):
        for y in range(width_y + 4):
            here = packed[x, y]
            value = here.astype(jnp.float32)
            after = jnp.where(row == pairs - 1, 0.0, pltpu.roll(value, pairs - 1, 0))
            before = jnp.where(row == 0, 0.0, pltpu.roll(value, 1, 0))
            windows[x, y, :, 0:LANES] = after.astype(jnp.bfloat16)
            windows[x, y, :, LANES : 2 * LANES] = here
            windows[x, y, :, 2 * LANES : 3 * LANES] = before.astype(jnp.bfloat16)
        return carry

    lax.fori_loop(0, width_x + 4, window, 0)

    halves_x, halves_y = width_x // 2, width_y // 2
    depth_k = (extent - 1) * HALF

    def step(i, totals):
        lhs = jnp.concatenate(
            [
                jnp.concatenate(
                    [
                        windows[2 * hx + 5 - i, 2 * hy + 5 - j]
                        for hx in range(halves_x)
                        for hy in range(halves_y)
                    ],
                    axis=0,
                )
                for j in range(extent - 1)
            ],
            axis=1,
        )
        out = []
        for py in range(2):
            rhs = jnp.concatenate(
                [
                    weights[i + px, py : py + extent - 1].reshape((extent - 1) * depth_k, LANES)
                    for px in range(2)
                ],
                axis=1,
            )
            out.append(totals[py] + jnp.dot(lhs, rhs, preferred_element_type=jnp.float32))
        return tuple(out)

    rows = halves_x * halves_y * pairs
    zero = jnp.zeros((rows, 2 * LANES), jnp.float32)
    totals = lax.fori_loop(0, extent - 1, step, (zero, zero))

    for py in range(2):
        for px in range(2):
            for hx in range(halves_x):
                for hy in range(halves_y):
                    start = (hx * halves_y + hy) * pairs
                    part = totals[py][start : start + pairs, px * LANES : (px + 1) * LANES]
                    x, y = 2 * hx + px, 2 * hy + py
                    boxes[1 + x, 1 + y] = part.astype(jnp.bfloat16)
                    mgrad_wide[x, y, pl.ds(0, pairs, stride=2), :] = part
                    mgrad_wide[x, y, pl.ds(1, pairs, stride=2), :] = pltpu.roll(part, HALF, 1)

    for k, (sx, sy) in enumerate(DIRS):
        @pl.when(exists(sx, sy))
        def _():
            exchange2(k).start()

    mgrad[...] = mgrad_wide[:, :, :, :coeffs]
    mgrad_copy = pltpu.make_async_copy(mgrad, mgrad_hbm, out_sem)
    mgrad_copy.start()

    chunk = 256
    own_rows = own_cols * pairs

    def turned(columns):
        return jnp.concatenate([boxes[x, y] for x, y in columns], axis=0).astype(jnp.float32).T.astype(
            jnp.bfloat16
        )

    def picks(base, size, at):
        local = (place[0:1, at] - base).astype(jnp.float32).astype(jnp.bfloat16)
        ids = lax.broadcasted_iota(jnp.int32, (size, chunk), 0).astype(jnp.bfloat16)
        return jnp.where(ids == local, jnp.bfloat16(1), jnp.bfloat16(0))

    def chosen(both, at):
        odd = place[1:2, at] == 1
        return jnp.where(odd, both[HALF:], both[:HALF])

    own = turned([(1 + x, 1 + y) for x in range(width_x) for y in range(width_y)])

    def pick_own(c, carry):
        at = pl.ds(pl.multiple_of(c * chunk, chunk), chunk)
        both = jnp.dot(own, picks(0, own_rows, at), preferred_element_type=jnp.float32)
        picked[:, at] = chosen(both, at)
        return carry

    lax.fori_loop(0, atoms // chunk, pick_own, 0)

    for k, (sx, sy) in enumerate(DIRS):
        @pl.when(exists(-sx, -sy))
        def _():
            exchange2(k).wait_recv()

    last_x, last_y = width_x + 1, width_y + 1
    ring = (
        [(0, 1 + y) for y in range(width_y)]
        + [(last_x, 1 + y) for y in range(width_y)]
        + [(1 + x, 0) for x in range(width_x)]
        + [(1 + x, last_y) for x in range(width_x)]
        + [(0, 0), (0, last_y), (last_x, 0), (last_x, last_y)]
    )
    outer = turned(ring)
    outer_rows = len(ring) * pairs
    basis_copy.wait()
    bgrad_copy.wait()

    def pick_outer(c, carry):
        at = pl.ds(pl.multiple_of(c * chunk, chunk), chunk)
        both = None
        for low in range(0, outer_rows, 256):
            size = min(256, outer_rows - low)
            term = jnp.dot(
                outer[:, low : low + size],
                picks(own_rows + low, size, at),
                preferred_element_type=jnp.float32,
            )
            both = term if both is None else both + term
        gathered = (picked[:, at] + chosen(both, at))[:coeffs]
        charge_ref[:, at] = jnp.sum(
            basis[:, at].astype(jnp.float32) * gathered, axis=0, keepdims=True
        )
        minus = -charges_ref[:, at]
        for a in range(3):
            forces_ref[a : a + 1, at] = minus * jnp.sum(
                bgrad[a, :, at].astype(jnp.float32) * gathered, axis=0, keepdims=True
            )
        return carry

    lax.fori_loop(0, atoms // chunk, pick_outer, 0)

    for k, (sx, sy) in enumerate(DIRS):
        @pl.when(exists(sx, sy))
        def _():
            exchange1(k).wait_send()
            exchange2(k).wait_send()
    mgrad_copy.wait()


def on_device(local_grad, translation, basis, basis_grad, charges, atom_leaf):
    coeffs, width_x, width_y, depth_z = local_grad.shape
    atoms = charges.shape[0]
    count_x, count_y = lax.axis_size("gx"), lax.axis_size("gy")
    extent = translation.shape[0]
    pairs = depth_z // 2
    grad = jnp.transpose(local_grad, (1, 2, 3, 0))
    block = (width_x, width_y, depth_z)
    f32, bf16 = jnp.float32, jnp.bfloat16

    def body(*refs):
        kernel(count_x, count_y, *refs)

    vmem = pl.BlockSpec(memory_space=pltpu.VMEM)
    hbm = pl.BlockSpec(memory_space=pl.ANY)
    dirs = len(DIRS)
    mgrad, charge_grad, forces = pl.pallas_call(
        body,
        out_shape=(
            jax.ShapeDtypeStruct(block + (coeffs,), f32),
            jax.ShapeDtypeStruct((1, atoms), f32),
            jax.ShapeDtypeStruct((3, atoms), f32),
        ),
        in_specs=[hbm, hbm, hbm, hbm, vmem, vmem],
        out_specs=(hbm, vmem, vmem),
        scratch_shapes=[
            pltpu.VMEM(block + (coeffs,), f32),
            pltpu.VMEM(block + (LANES,), f32),
            pltpu.VMEM(translation.shape, bf16),
            pltpu.VMEM(basis.shape, bf16),
            pltpu.VMEM(basis_grad.shape, bf16),
            pltpu.VMEM((width_x + 4, width_y + 4, pairs, LANES), bf16),
            pltpu.VMEM((width_x + 4, width_y + 4, pairs, 3 * LANES), bf16),
            pltpu.VMEM((extent, extent, (extent - 1) * HALF, LANES), bf16),
            pltpu.VMEM(block + (LANES,), f32),
            pltpu.VMEM(block + (coeffs,), f32),
            pltpu.VMEM((width_x + 2, width_y + 2, pairs, LANES), bf16),
            pltpu.VMEM((HALF, atoms), f32),
            pltpu.VMEM((8, atoms), jnp.int32),
            pltpu.SemaphoreType.DMA((3,)),
            pltpu.SemaphoreType.DMA((extent,)),
            pltpu.SemaphoreType.DMA((dirs,)),
            pltpu.SemaphoreType.DMA((dirs,)),
            pltpu.SemaphoreType.DMA((dirs,)),
            pltpu.SemaphoreType.DMA((dirs,)),
            pltpu.SemaphoreType.DMA,
        ],
        compiler_params=pltpu.CompilerParams(
            collective_id=0, has_side_effects=True, vmem_limit_bytes=48 * 2**20
        ),
        name="far_adjoint",
    )(grad, translation, basis, basis_grad, charges[None], atom_leaf[None])
    return (jnp.transpose(mgrad, (3, 0, 1, 2)), charge_grad[0], forces)


def solution(mesh):
    in_specs = (
        P(None, ("groups", "gx"), "gy", None),
        P(),
        P(None, ("groups", "gx", "gy")),
        P(None, None, ("groups", "gx", "gy")),
        P(("groups", "gx", "gy")),
        P(("groups", "gx", "gy")),
    )
    out_specs = (
        P(None, ("groups", "gx"), "gy", None),
        P(("groups", "gx", "gy")),
        P(None, ("groups", "gx", "gy")),
    )
    return jax.shard_map(
        on_device, mesh=mesh, in_specs=in_specs, out_specs=out_specs, check_vma=False
    )
```

```python
import jax
import jax.numpy as jnp
from jax import lax
from jax.experimental import pallas as pl
from jax.experimental.pallas import tpu as pltpu
from jax.sharding import PartitionSpec as P

MESH = pl.DeviceIdType.MESH
LANES = 128
HALF = 64
CHUNK = 256
VMEM_LIMIT = 58 * 2**20
DIRS = ((-1, 0), (1, 0), (0, -1), (0, 1), (-1, -1), (-1, 1), (1, -1), (1, 1))


def source_span(step, width, depth):
    if step == 0:
        return depth, width
    return (depth, depth) if step < 0 else (width, depth)


def target_span(step, width, depth):
    if step == 0:
        return depth, width
    return (width + depth, depth) if step < 0 else (0, depth)


def split(value, size):
    if size & (size - 1) == 0:
        return value >> (size.bit_length() - 1), value & (size - 1)
    quotient = lax.div(value, jnp.int32(size))
    return quotient, value - quotient * size


def picks(place, rows, base, size):
    index = jnp.concatenate([place[pl.ds(r, 1), :] for r in rows], axis=1) >> 1
    local = (index - base).astype(jnp.float32).astype(jnp.bfloat16)
    ids = lax.broadcasted_iota(jnp.int32, (size, local.shape[1]), 0).astype(jnp.bfloat16)
    return jnp.where(ids == local, jnp.bfloat16(1), jnp.bfloat16(0))


def chosen(both, place, rows):
    odd = jnp.concatenate([place[pl.ds(r, 1), :] for r in rows], axis=1) & 1
    return jnp.where(odd == 1, both[HALF:], both[:HALF])


def kernel(
    count_x,
    count_y,
    grad_hbm,
    trans_hbm,
    leaf_hbm,
    mgrad,
    outer,
    picked,
    place,
    grad,
    wide,
    trans,
    leaf_in,
    packed,
    windows,
    weights,
    mgrad_wide,
    boxes,
    load_sem,
    trans_sem,
    send_sem,
    recv_sem,
    send2_sem,
    recv2_sem,
):
    width_x, width_y, depth_z, coeffs = grad.shape
    pairs = depth_z // 2
    extent = trans.shape[0]
    atoms = picked.shape[1]
    gx, gy = lax.axis_index("gx"), lax.axis_index("gy")

    grad_copy = pltpu.make_async_copy(grad_hbm, grad, load_sem.at[0])
    grad_copy.start()
    for dx in range(extent):
        pltpu.make_async_copy(trans_hbm.at[dx], trans.at[dx], trans_sem.at[dx]).start()
    leaf_copy = pltpu.make_async_copy(leaf_hbm, leaf_in, load_sem.at[1])
    leaf_copy.start()

    def exists(sx, sy):
        ok = None
        for here, step, count in ((gx, sx, count_x), (gy, sy, count_y)):
            if step:
                test = (here + step >= 0) & (here + step < count)
                ok = test if ok is None else ok & test
        return ok

    barrier = pltpu.get_barrier_semaphore()
    for sx, sy in DIRS:
        @pl.when(exists(sx, sy))
        def _():
            pl.semaphore_signal(
                barrier, inc=1, device_id={"gx": gx + sx, "gy": gy + sy}, device_id_type=MESH
            )

    def spans(which, sx, sy, depth):
        (x0, nx), (y0, ny) = which(sx, width_x, depth), which(sy, width_y, depth)
        return pl.ds(x0, nx), pl.ds(y0, ny)

    def exchange1(k):
        sx, sy = DIRS[k]
        src = spans(source_span, sx, sy, 2)
        dst = spans(target_span, sx, sy, 2)
        return pltpu.make_async_remote_copy(
            src_ref=packed.at[src[0], src[1]],
            dst_ref=packed.at[dst[0], dst[1]],
            send_sem=send_sem.at[k],
            recv_sem=recv_sem.at[k],
            device_id={"gx": gx + sx, "gy": gy + sy},
            device_id_type=MESH,
        )

    def exchange2(k):
        sx, sy = DIRS[k]
        src = spans(source_span, sx, sy, 1)
        dst = spans(target_span, sx, sy, 1)
        return pltpu.make_async_remote_copy(
            src_ref=boxes.at[src[0], src[1]],
            dst_ref=boxes.at[dst[0], dst[1]],
            send_sem=send2_sem.at[k],
            recv_sem=recv2_sem.at[k],
            device_id={"gx": gx + sx, "gy": gy + sy},
            device_id_type=MESH,
        )

    wide[...] = jnp.zeros_like(wide)
    grad_copy.wait()
    wide[:, :, :, :coeffs] = grad[...]
    for x in range(width_x):
        for y in range(width_y):
            even = wide[x, y, pl.ds(0, pairs, stride=2), :]
            odd = wide[x, y, pl.ds(1, pairs, stride=2), :]
            both = odd + pltpu.roll(even, HALF, 1)
            packed[2 + x, 2 + y] = both.astype(jnp.bfloat16)

    def span_of(here, count):
        return jnp.minimum(here + 1, count - 1) - jnp.maximum(here - 1, 0) + 1

    pl.semaphore_wait(barrier, span_of(gx, count_x) * span_of(gy, count_y) - 1)

    for k, (sx, sy) in enumerate(DIRS):
        @pl.when(exists(sx, sy))
        def _():
            exchange1(k).start()

        @pl.when(jnp.logical_not(exists(sx, sy)))
        def _():
            x, y = spans(target_span, -sx, -sy, 2)
            packed[x, y] = jnp.zeros((x.size, y.size, pairs, LANES), jnp.bfloat16)
            x, y = spans(target_span, -sx, -sy, 1)
            boxes[x, y] = jnp.zeros((x.size, y.size, pairs, LANES), jnp.bfloat16)

    leaf_copy.wait()
    leaf = leaf_in[...]
    rest, z = split(leaf, depth_z)
    lx, ly = split(rest, width_y * count_y)
    lx, ly = lx - gx * width_x, ly - gy * width_y
    in_x = (lx >= 0) & (lx < width_x)
    in_y = (ly >= 0) & (ly < width_y)
    own_cols = width_x * width_y
    face_x = jnp.where(lx < 0, 0, width_y) + ly
    face_y = 2 * width_y + jnp.where(ly < 0, 0, width_x) + lx
    corner = 2 * (width_x + width_y) + jnp.where(lx < 0, 0, 2) + jnp.where(ly < 0, 0, 1)
    column = jnp.where(
        in_x & in_y,
        lx * width_y + ly,
        own_cols + jnp.where(in_y, face_x, jnp.where(in_x, face_y, corner)),
    )
    place[...] = column * depth_z + z

    def prepare(dx, carry):
        pltpu.make_async_copy(trans_hbm.at[dx], trans.at[dx], trans_sem.at[dx]).wait()
        for dy in range(extent):
            blocks = []
            for dz in range(extent):
                one = trans[dx, dy, dz]
                blocks.append(jnp.pad(one, ((0, HALF - coeffs), (0, HALF - coeffs))))
            for m in range(extent - 1):
                weights[dx, dy, m * HALF : (m + 1) * HALF, :] = jnp.concatenate(
                    [blocks[m], blocks[m + 1]], axis=1
                )
        return carry

    lax.fori_loop(0, extent, prepare, 0)
    low_lanes = lax.broadcasted_iota(jnp.int32, (HALF, LANES), 1) < HALF
    for dx in range(2, extent - 2):
        for dy in range(2, extent - 2):
            first, last = pl.ds(HALF, HALF), pl.ds(4 * HALF, HALF)
            head = weights[dx, dy, first, :].astype(jnp.float32)
            weights[dx, dy, first, :] = jnp.where(low_lanes, head, 0.0).astype(jnp.bfloat16)
            weights[dx, dy, pl.ds(2 * HALF, 2 * HALF), :] = jnp.zeros(
                (2 * HALF, LANES), jnp.bfloat16
            )
            tail = weights[dx, dy, last, :].astype(jnp.float32)
            weights[dx, dy, last, :] = jnp.where(low_lanes, 0.0, tail).astype(jnp.bfloat16)

    for k, (sx, sy) in enumerate(DIRS):
        @pl.when(exists(-sx, -sy))
        def _():
            exchange1(k).wait_recv()

    row = lax.broadcasted_iota(jnp.int32, (pairs, LANES), 0)

    def window(x, carry):
        for y in range(width_y + 4):
            here = packed[x, y]
            value = here.astype(jnp.float32)
            after = jnp.where(row == pairs - 1, 0.0, pltpu.roll(value, pairs - 1, 0))
            before = jnp.where(row == 0, 0.0, pltpu.roll(value, 1, 0))
            windows[x, y, :, 0:LANES] = after.astype(jnp.bfloat16)
            windows[x, y, :, LANES : 2 * LANES] = here
            windows[x, y, :, 2 * LANES : 3 * LANES] = before.astype(jnp.bfloat16)
        return carry

    lax.fori_loop(0, width_x + 4, window, 0)

    halves_x, halves_y = width_x // 2, width_y // 2
    depth_k = (extent - 1) * HALF

    def step(i, totals):
        lhs = jnp.concatenate(
            [
                jnp.concatenate(
                    [
                        windows[2 * hx + 5 - i, 2 * hy + 5 - j]
                        for hx in range(halves_x)
                        for hy in range(halves_y)
                    ],
                    axis=0,
                )
                for j in range(extent - 1)
            ],
            axis=1,
        )
        out = []
        for py in range(2):
            rhs = jnp.concatenate(
                [
                    weights[i + px, py : py + extent - 1].reshape((extent - 1) * depth_k, LANES)
                    for px in range(2)
                ],
                axis=1,
            )
            out.append(totals[py] + jnp.dot(lhs, rhs, preferred_element_type=jnp.float32))
        return tuple(out)

    rows = halves_x * halves_y * pairs
    zero = jnp.zeros((rows, 2 * LANES), jnp.float32)
    totals = lax.fori_loop(0, extent - 1, step, (zero, zero), unroll=True)

    for py in range(2):
        for px in range(2):
            for hx in range(halves_x):
                for hy in range(halves_y):
                    start = (hx * halves_y + hy) * pairs
                    part = totals[py][start : start + pairs, px * LANES : (px + 1) * LANES]
                    x, y = 2 * hx + px, 2 * hy + py
                    boxes[1 + x, 1 + y] = part.astype(jnp.bfloat16)
                    mgrad_wide[x, y, pl.ds(0, pairs, stride=2), :] = part
                    mgrad_wide[x, y, pl.ds(1, pairs, stride=2), :] = pltpu.roll(part, HALF, 1)

    for k, (sx, sy) in enumerate(DIRS):
        @pl.when(exists(sx, sy))
        def _():
            exchange2(k).start()

    mgrad[...] = mgrad_wide[:, :, :, :coeffs]
    own_rows = own_cols * pairs

    def turned(columns):
        return jnp.concatenate([boxes[x, y] for x, y in columns], axis=0).astype(jnp.float32).T.astype(
            jnp.bfloat16
        )

    own = turned([(1 + x, 1 + y) for x in range(width_x) for y in range(width_y)])

    def pick_own(c, carry):
        at = pl.ds(pl.multiple_of(c * CHUNK, CHUNK), CHUNK)
        rows = [c * (CHUNK // LANES) + r for r in range(CHUNK // LANES)]
        both = jnp.dot(
            own, picks(place, rows, 0, own_rows), preferred_element_type=jnp.float32
        )
        picked[:, at] = chosen(both, place, rows).astype(jnp.bfloat16)
        return carry

    lax.fori_loop(0, atoms // CHUNK, pick_own, 0, unroll=4)

    for k, (sx, sy) in enumerate(DIRS):
        @pl.when(exists(-sx, -sy))
        def _():
            exchange2(k).wait_recv()

    last_x, last_y = width_x + 1, width_y + 1
    ring = (
        [(0, 1 + y) for y in range(width_y)]
        + [(last_x, 1 + y) for y in range(width_y)]
        + [(1 + x, 0) for x in range(width_x)]
        + [(1 + x, last_y) for x in range(width_x)]
        + [(0, 0), (0, last_y), (last_x, 0), (last_x, last_y)]
    )
    outer[...] = turned(ring)

    for k, (sx, sy) in enumerate(DIRS):
        @pl.when(exists(sx, sy))
        def _():
            exchange1(k).wait_send()
            exchange2(k).wait_send()


def tail(
    own_rows,
    mgrad_in,
    outer_hbm,
    picked_hbm,
    place_hbm,
    basis,
    bgrad,
    charges,
    mgrad_hbm,
    charge_ref,
    forces_ref,
    outer,
    picked,
    place,
    mgrad,
    load_sem,
    out_sem,
):
    coeffs, atoms = basis.shape
    loads = [
        pltpu.make_async_copy(source, target, load_sem.at[k])
        for k, (source, target) in enumerate(
            ((mgrad_in, mgrad), (place_hbm, place), (outer_hbm, outer), (picked_hbm, picked))
        )
    ]
    for load in loads:
        load.start()
    for load in loads:
        load.wait()
    mgrad_copy = pltpu.make_async_copy(mgrad, mgrad_hbm, out_sem)
    mgrad_copy.start()
    outer_rows = outer.shape[1]

    def pick_outer(c, carry):
        at = pl.ds(pl.multiple_of(c * CHUNK, CHUNK), CHUNK)
        rows = [c * (CHUNK // LANES) + r for r in range(CHUNK // LANES)]
        both = None
        for low in range(0, outer_rows, 256):
            size = min(256, outer_rows - low)
            term = jnp.dot(
                outer[:, low : low + size],
                picks(place, rows, own_rows + low, size),
                preferred_element_type=jnp.float32,
            )
            both = term if both is None else both + term
        gathered = (picked[:, at].astype(jnp.float32) + chosen(both, place, rows))[:coeffs]
        charge_ref[:, at] = jnp.sum(
            basis[:, at].astype(jnp.float32) * gathered, axis=0, keepdims=True
        )
        minus = -charges[:, at]
        for a in range(3):
            forces_ref[a : a + 1, at] = minus * jnp.sum(
                bgrad[a, :, at].astype(jnp.float32) * gathered, axis=0, keepdims=True
            )
        return carry

    lax.fori_loop(0, atoms // CHUNK, pick_outer, 0, unroll=4)
    mgrad_copy.wait()


def on_device(local_grad, translation, basis, basis_grad, charges, atom_leaf):
    coeffs, width_x, width_y, depth_z = local_grad.shape
    atoms = charges.shape[0]
    count_x, count_y = lax.axis_size("gx"), lax.axis_size("gy")
    extent = translation.shape[0]
    pairs = depth_z // 2
    outer_rows = (2 * (width_x + width_y) + 4) * pairs
    grad = jnp.transpose(local_grad, (1, 2, 3, 0))
    block = (width_x, width_y, depth_z)
    f32, bf16 = jnp.float32, jnp.bfloat16

    def body(*refs):
        kernel(count_x, count_y, *refs)

    def tail_body(*refs):
        tail(width_x * width_y * pairs, *refs)

    vmem = pl.BlockSpec(memory_space=pltpu.VMEM)
    hbm = pl.BlockSpec(memory_space=pltpu.HBM)
    dirs = len(DIRS)
    mgrad, outer, picked, place = pl.pallas_call(
        body,
        out_shape=(
            jax.ShapeDtypeStruct(block + (coeffs,), f32),
            jax.ShapeDtypeStruct((LANES, outer_rows), bf16),
            jax.ShapeDtypeStruct((HALF, atoms), bf16),
            jax.ShapeDtypeStruct((atoms // LANES, LANES), jnp.int32),
        ),
        in_specs=[hbm, hbm, hbm],
        out_specs=(vmem, vmem, vmem, vmem),
        scratch_shapes=[
            pltpu.VMEM(block + (coeffs,), f32),
            pltpu.VMEM(block + (LANES,), f32),
            pltpu.VMEM(translation.shape, bf16),
            pltpu.VMEM((atoms // LANES, LANES), jnp.int32),
            pltpu.VMEM((width_x + 4, width_y + 4, pairs, LANES), bf16),
            pltpu.VMEM((width_x + 4, width_y + 4, pairs, 3 * LANES), bf16),
            pltpu.VMEM((extent, extent, (extent - 1) * HALF, LANES), bf16),
            pltpu.VMEM(block + (LANES,), f32),
            pltpu.VMEM((width_x + 2, width_y + 2, pairs, LANES), bf16),
            pltpu.SemaphoreType.DMA((2,)),
            pltpu.SemaphoreType.DMA((extent,)),
            pltpu.SemaphoreType.DMA((dirs,)),
            pltpu.SemaphoreType.DMA((dirs,)),
            pltpu.SemaphoreType.DMA((dirs,)),
            pltpu.SemaphoreType.DMA((dirs,)),
        ],
        compiler_params=pltpu.CompilerParams(
            collective_id=0, has_side_effects=True, vmem_limit_bytes=VMEM_LIMIT
        ),
        name="far_adjoint",
    )(grad, translation, atom_leaf.reshape(atoms // LANES, LANES))
    mgrad, charge_grad, forces = pl.pallas_call(
        tail_body,
        out_shape=(
            jax.ShapeDtypeStruct(block + (coeffs,), f32),
            jax.ShapeDtypeStruct((1, atoms), f32),
            jax.ShapeDtypeStruct((3, atoms), f32),
        ),
        in_specs=[hbm] * 4 + [vmem] * 3,
        out_specs=(hbm, vmem, vmem),
        scratch_shapes=[
            pltpu.VMEM((LANES, outer_rows), bf16),
            pltpu.VMEM((HALF, atoms), bf16),
            pltpu.VMEM((atoms // LANES, LANES), jnp.int32),
            pltpu.VMEM(block + (coeffs,), f32),
            pltpu.SemaphoreType.DMA((4,)),
            pltpu.SemaphoreType.DMA,
        ],
        compiler_params=pltpu.CompilerParams(vmem_limit_bytes=VMEM_LIMIT),
        name="atom_sums",
    )(mgrad, outer, picked, place, basis, basis_grad, charges[None])
    return (jnp.transpose(mgrad, (3, 0, 1, 2)), charge_grad[0], forces)


def solution(mesh):
    in_specs = (
        P(None, ("groups", "gx"), "gy", None),
        P(),
        P(None, ("groups", "gx", "gy")),
        P(None, None, ("groups", "gx", "gy")),
        P(("groups", "gx", "gy")),
        P(("groups", "gx", "gy")),
    )
    out_specs = (
        P(None, ("groups", "gx"), "gy", None),
        P(("groups", "gx", "gy")),
        P(None, ("groups", "gx", "gy")),
    )
    return jax.shard_map(
        on_device, mesh=mesh, in_specs=in_specs, out_specs=out_specs, check_vma=False
    )
```
